256 devices in a mesh: ia: 16 (over x, z_hi, core), ja: 4 (over z_lo), ka: 4 (over y).
Axes of the slice: x: 4, y: 4, z: 8 (z_hi: 2, z_lo: 4; z = z_hi * 4 + z_lo), core: 2. Of those that a mesh axis runs over, the one named last changes fastest.
Arguments:
- blocks: bfloat16 [16, 4, 4, 3, 128, 128, 128], P('ia', 'ja', 'ka'), may hold values from -6 to 6
- coords: int32 [16, 4, 4, 3, 3], P('ia', 'ja', 'ka'), may hold values from 0 to 3
- counts: int32 [16, 4, 4], P('ia', 'ja', 'ka'), may hold values from 1 to 3, as said below
- b_factor: float32 [4, 512, 256], P('ja', ('ia', 'ka')), may hold values from -50 to 100
- c_factor: float32 [4, 512, 256], P('ka', ('ia', 'ja')), may hold values from -50 to 100
Outputs:
- a_new: float32 [16, 512, 256], P('ia', ('ja', 'ka'))
- b_new: float32 [4, 512, 256], P('ja', ('ia', 'ka'))
The draws below stay inside these ranges and needn't reach their ends.
Inputs may be any that keep to these rules, and one draw needn't show every extreme that they name: Only the first counts slots of a cell hold live blocks; the other slots are ignored. Some cell is full in every draw. `coords`: row blocks are local to the cell's slab of each mode; one cell may name the same row block in several slots.
All inputs are finite; a program needn't handle non-finite values.
Results may differ from the reference program's by a relative error of at most 0.007.
Values may be sent and summed in bfloat16 or wider, within the bound.
No kernel may reach another device: no remote copies, remote signals or barrier semaphores. Data moves between devices by JAX's collectives and lax.ppermute only.
A program may use at most 128 MiB of HBM per device.

```python
import jax
import jax.numpy as jnp
from jax import lax

BS = 128
R = 256
RB = 4
NBLK = 3
SLAB = 512
NA = 8192
NB = 2048
NC = 2048
N_IA = 16
N_JA = 4
N_KA = 4


def draw_counts(key, part):
    first_key, second_key = jax.random.split(key)
    cell_total = N_IA * N_JA * N_KA
    picks = jax.random.randint(first_key, (cell_total,), 0, 4)
    filled = jnp.where(picks == 0, NBLK, 1).astype(jnp.int32)
    chosen = jax.random.randint(second_key, (), 0, cell_total)
    positions = jnp.arange(cell_total, dtype=jnp.int32)
    filled = jnp.where(positions == chosen, NBLK, filled).astype(jnp.int32)
    return filled.reshape(N_IA, N_JA, N_KA)


def factor_rows(key, slabs):
    scale_key, entry_key = jax.random.split(key)
    lows = jax.random.uniform(scale_key, (slabs, SLAB, 1), jnp.float32, 0.02, 1.0)
    row_scales = 1.0 / lows
    entries = jax.random.uniform(entry_key, (slabs, SLAB, R), jnp.float32, -1.0, 2.0)
    return (entries * row_scales).astype(jnp.float32)


def draw_b_factor(key, part):
    key = jax.random.fold_in(key, 11)
    return factor_rows(key, N_JA)


def draw_c_factor(key, part):
    key = jax.random.fold_in(key, 23)
    return factor_rows(key, N_KA)


def place_ends(array, stream_key, low, largest):
    place = [jax.random.randint(jax.random.fold_in(stream_key, axis), (), 0, length) for axis, length in enumerate(array.shape)]
    longest = array.shape.index(max(array.shape))
    next_to = place[:longest] + [(place[longest] + 1) % array.shape[longest]] + place[longest + 1:]
    return array.at[tuple(place)].set(low).at[tuple(next_to)].set(largest)


def steps_of(stream_key, dims, cuts, smallest, high):
    def one(dim, blocks):
        steps = jax.random.uniform(jax.random.fold_in(jax.random.fold_in(stream_key, 6), dim), (blocks,), jnp.float32, smallest / len(cuts), high / len(cuts))
        return jnp.repeat(jnp.exp(steps), dims[dim] // blocks).reshape((-1,) + (1,) * (len(dims) - dim - 1))

    gain = one(*cuts[0])
    for cut in cuts[1:]:
        gain = gain * one(*cut)
    return gain


def noise(key, extent, scale, reach, pieces=(), kind=jnp.bfloat16):
    values = scale * jax.random.normal(key, extent, jnp.float32)
    if pieces:
        values = values * steps_of(key, extent, pieces, -0.22, 0.18)
    return jnp.clip(values, -reach, reach).astype(kind)


def setup_inputs(seed: int = 0) -> dict:
    keys = jax.random.split(jax.random.key(seed), 6)
    return {
        "blocks": noise(keys[0], (N_IA, N_JA, N_KA, NBLK, BS, BS, BS), 1.0, 6.0, ((0, 16), (1, 4), (2, 4))),
        "coords": place_ends(jax.random.randint(keys[1], (N_IA, N_JA, N_KA, NBLK, 3), 0, RB), jax.random.fold_in(keys[1], 1), 0, RB - 1).astype(jnp.int32),
        "counts": draw_counts(jax.random.fold_in(keys[5], 71), 0),
        "b_factor": draw_b_factor(jax.random.fold_in(keys[5], 71), 0),
        "c_factor": draw_c_factor(jax.random.fold_in(keys[5], 71), 0),
    }


def solve_right(matrix, hadamard):
    factor_low = jnp.linalg.cholesky(hadamard)
    partial_solve = lax.linalg.triangular_solve(factor_low, matrix, left_side=False, lower=True, transpose_a=True)
    return lax.linalg.triangular_solve(factor_low, partial_solve, left_side=False, lower=True, transpose_a=False)

def unit_columns(unscaled):
    scale_cols = jnp.sqrt(lax.optimization_barrier(jnp.mean(unscaled * unscaled, axis=0)) + 1e-06)
    return unscaled / scale_cols

def reference(blocks, coords, counts, b_factor, c_factor):
    rank_width = b_factor.shape[2]
    cell_total = N_IA * N_JA * N_KA
    b_rows = b_factor.reshape(NB, rank_width)
    c_rows = c_factor.reshape(NC, rank_width)
    gram_b = jnp.dot(b_rows.T.astype(jnp.float32), b_rows.astype(jnp.float32), precision=lax.Precision.HIGHEST, preferred_element_type=jnp.float32) / NB
    gram_c = jnp.dot(c_rows.T.astype(jnp.float32), c_rows.astype(jnp.float32), precision=lax.Precision.HIGHEST, preferred_element_type=jnp.float32) / NC
    b_half = b_rows.astype(jnp.bfloat16)
    c_half = c_rows.astype(jnp.bfloat16)
    flat_blocks = blocks.reshape(cell_total * NBLK, BS, BS, BS)
    flat_coords = coords.reshape(cell_total * NBLK, 3).astype(jnp.int32)
    flat_counts = counts.reshape(cell_total).astype(jnp.int32)
    slot_ids = jnp.arange(cell_total * NBLK, dtype=jnp.int32)

    def locate(slot_index):
        cell_index = slot_index // NBLK
        index_i = cell_index // (N_JA * N_KA)
        index_j = cell_index // N_KA % N_JA
        index_k = cell_index % N_KA
        live_flag = slot_index % NBLK < flat_counts[cell_index]
        return (index_i, index_j, index_k, live_flag)

    def product(slot_index, index_k):
        tensor_block = lax.dynamic_index_in_dim(flat_blocks, slot_index, 0, keepdims=False)
        c_start = (index_k * SLAB + flat_coords[slot_index, 2] * BS).astype(jnp.int32)
        c_block = lax.dynamic_slice_in_dim(c_half, c_start, BS, 0)
        flat_prod = jnp.dot(tensor_block.reshape(BS * BS, BS).astype(jnp.float32), c_block.astype(jnp.float32), precision=lax.Precision.HIGHEST, preferred_element_type=jnp.float32)
        return flat_prod.astype(jnp.bfloat16).reshape(BS, BS, rank_width)

    def mode_one(summed, slot_index):
        index_i, index_j, index_k, live_flag = locate(slot_index)

        def accumulate(summed_in):
            product_block = product(slot_index, index_k).astype(jnp.float32)
            b_start = (index_j * SLAB + flat_coords[slot_index, 1] * BS).astype(jnp.int32)
            b_block = lax.dynamic_slice_in_dim(b_half, b_start, BS, 0).astype(jnp.float32)
            contrib = jnp.einsum('pqr,qr->pr', product_block, b_block, precision=lax.Precision.HIGHEST)
            row_start = (index_i * SLAB + flat_coords[slot_index, 0] * BS).astype(jnp.int32)
            previous = lax.dynamic_slice_in_dim(summed_in, row_start, BS, 0)
            return lax.dynamic_update_slice_in_dim(summed_in, previous + contrib, row_start, 0)
        return (lax.cond(live_flag, accumulate, lambda value: value, summed), None)
    m_a, _ = lax.scan(mode_one, jnp.zeros((NA, rank_width), jnp.float32), slot_ids)
    a_new = unit_columns(solve_right(m_a, gram_b * gram_c))
    gram_a = jnp.dot(a_new.T.astype(jnp.float32), a_new.astype(jnp.float32), precision=lax.Precision.HIGHEST, preferred_element_type=jnp.float32) / NA
    a_half = a_new.astype(jnp.bfloat16)

    def mode_two(summed, slot_index):
        index_i, index_j, index_k, live_flag = locate(slot_index)

        def accumulate(summed_in):
            product_block = product(slot_index, index_k).astype(jnp.float32)
            a_start = (index_i * SLAB + flat_coords[slot_index, 0] * BS).astype(jnp.int32)
            a_block = lax.dynamic_slice_in_dim(a_half, a_start, BS, 0).astype(jnp.float32)
            contrib = jnp.einsum('pqr,pr->qr', product_block, a_block, precision=lax.Precision.HIGHEST)
            row_start = (index_j * SLAB + flat_coords[slot_index, 1] * BS).astype(jnp.int32)
            previous = lax.dynamic_slice_in_dim(summed_in, row_start, BS, 0)
            return lax.dynamic_update_slice_in_dim(summed_in, previous + contrib, row_start, 0)
        return (lax.cond(live_flag, accumulate, lambda value: value, summed), None)
    m_b, _ = lax.scan(mode_two, jnp.zeros((NB, rank_width), jnp.float32), slot_ids)
    b_new = unit_columns(solve_right(m_b, gram_a * gram_c))
    return (a_new.reshape(N_IA, SLAB, rank_width), b_new.reshape(N_JA, SLAB, rank_width))
```

```python
import functools

import jax
import jax.numpy as jnp
from jax import lax
from jax.experimental import pallas as pl
from jax.experimental.pallas import tpu as pltpu
from jax.sharding import PartitionSpec as P

NX, NH, NC, NJ, NK = 4, 2, 2, 4, 4
AXES = ("ia", "ja", "ka")
F32, BF16 = jnp.float32, jnp.bfloat16
CHUNK = 16
EDGE = 32


def flat_index(place):
    x, h, c, j, k = place
    return (((x * NH + h) * NC + c) * NJ + j) * NK + k


PLACES = [
    (x, h, c, j, k)
    for x in range(NX)
    for h in range(NH)
    for c in range(NC)
    for j in range(NJ)
    for k in range(NK)
]


def send(value, move):
    return lax.ppermute(value, AXES, [(flat_index(p), flat_index(move(p))) for p in PLACES])


def flip_core(p):
    return (p[0], p[1], 1 - p[2], p[3], p[4])


def flip_half(p):
    return (p[0], 1 - p[1], p[2], p[3], p[4])


def along_x(s, p):
    return ((p[0] + s) % NX, p[1], p[2], p[3], p[4])


def along_j(s, p):
    return (p[0], p[1], p[2], (p[3] + s) % NJ, p[4])


def along_k(s, p):
    return (p[0], p[1], p[2], p[3], (p[4] + s) % NK)


def k_or_j(s, p):
    return along_k(s, p) if p[2] == 0 else along_j(s, p)


def j_or_k(s, p):
    return along_j(s, p) if p[2] == 0 else along_k(s, p)


def ring_shifts(value, move):
    return [value] + [send(value, functools.partial(move, s)) for s in (1, 2, 3)]


def ring_gather(value, move, me, axis=0):
    got = ring_shifts(value, move)
    return jnp.stack([lax.select_n(lax.rem(me - t + 4, 4), *got) for t in range(4)], axis)


def ring_sum(value, move):
    got = ring_shifts(value, move)
    return (got[0] + got[1]) + (got[2] + got[3])


def ring_scatter(value, move, me):
    part = lambda s: lax.dynamic_index_in_dim(value, lax.rem(me + s, 4), 0, keepdims=False)
    got = [send(part(s), functools.partial(move, s)) for s in (1, 2, 3)]
    return (part(0) + got[0]) + (got[1] + got[2])


def dot_full(a, b):
    return jnp.dot(a, b, precision=lax.Precision.HIGHEST, preferred_element_type=F32)


def gram_of(rows):
    return lax.dot_general(
        rows, rows, (((0,), (0,)), ((), ())),
        precision=lax.Precision.HIGHEST, preferred_element_type=F32,
    )


def small_inverse(d):
    n = d.shape[0]
    lane = lax.broadcasted_iota(jnp.int32, d.shape, 1)
    sub = lax.broadcasted_iota(jnp.int32, d.shape, 0)
    for k in range(n):
        col = jnp.broadcast_to(d[:, k : k + 1], d.shape)
        pivot = 1.0 / col[k : k + 1, :]
        row = jnp.where(lane[:1] == k, pivot, d[k : k + 1, :] * pivot)
        d = jnp.where(sub == k, row, jnp.where(lane == k, 0.0, d) - col * row)
    return d


def inverse_body(h_ref, out_ref):
    n = h_ref.shape[0]
    out_ref[...] = h_ref[...]
    for s in range(0, n, EDGE):
        block = slice(s, s + EDGE)
        inv = small_inverse(out_ref[block, block])
        panel = out_ref[:, block]
        row = dot_full(inv, out_ref[block, :])
        out_ref[...] = out_ref[...] - dot_full(panel, row)
        out_ref[:, block] = -dot_full(panel, inv)
        out_ref[block, :] = row
        out_ref[block, block] = inv


def spd_inverse(h):
    n = h.shape[0]
    return pl.pallas_call(
        inverse_body,
        out_shape=jax.ShapeDtypeStruct((n, n), F32),
        in_specs=[pl.BlockSpec(memory_space=pltpu.VMEM)],
        out_specs=pl.BlockSpec(memory_space=pltpu.VMEM),
        cost_estimate=pl.CostEstimate(flops=2 * n**3, bytes_accessed=8 * n * n, transcendentals=0),
        name="spd_inverse",
    )(h)


def block_specs(slots, size, rank, slab):
    chunks = size // CHUNK

    def pick(n, p, count, coords):
        live = n < count[0]
        return (jnp.minimum(n, count[0] - 1), jnp.where(live, p, chunks - 1), 0, 0)

    whole = pl.BlockSpec((slab, rank), lambda n, p, count, coords: (0, 0))
    return chunks, pl.BlockSpec((1, CHUNK, size, size), pick), whole


def mode_one_body(count, coords, x_ref, b_ref, c_ref, out_ref):
    n, p = pl.program_id(0), pl.program_id(1)
    size = x_ref.shape[-1]
    rank = c_ref.shape[-1]

    @pl.when((n == 0) & (p == 0))
    def _():
        out_ref[...] = jnp.zeros_like(out_ref)

    @pl.when(n < count[0])
    def _():
        c_rows = c_ref[pl.ds(pl.multiple_of(coords[n, 2] * size, size), size), :]
        b_rows = b_ref[pl.ds(pl.multiple_of(coords[n, 1] * size, size), size), :].astype(F32)
        x = x_ref[0].reshape(CHUNK * size, size)
        prod = jnp.dot(x, c_rows, preferred_element_type=F32).astype(BF16).astype(F32)
        part = jnp.sum(prod.reshape(CHUNK, size, rank) * b_rows[None], axis=1)
        rows = pl.ds(pl.multiple_of(coords[n, 0] * size + p * CHUNK, CHUNK), CHUNK)
        out_ref[rows, :] += part


def mode_two_body(count, coords, x_ref, a_ref, c_ref, out_ref):
    n, p = pl.program_id(0), pl.program_id(1)
    size = x_ref.shape[-1]
    rank = c_ref.shape[-1]

    @pl.when((n == 0) & (p == 0))
    def _():
        out_ref[...] = jnp.zeros_like(out_ref)

    @pl.when(n < count[0])
    def _():
        c_rows = c_ref[pl.ds(pl.multiple_of(coords[n, 2] * size, size), size), :]
        a_rows = a_ref[pl.ds(pl.multiple_of(coords[n, 0] * size + p * CHUNK, CHUNK), CHUNK), :]
        x = x_ref[0].reshape(CHUNK * size, size)
        prod = jnp.dot(x, c_rows, preferred_element_type=F32).astype(BF16).astype(F32)
        part = jnp.sum(prod.reshape(CHUNK, size, rank) * a_rows.astype(F32)[:, None, :], axis=0)
        rows = pl.ds(pl.multiple_of(coords[n, 1] * size, size), size)
        out_ref[rows, :] += part


def mode_update(body, count, coords, blocks, factor, c_slab, name):
    slots, size = blocks.shape[0], blocks.shape[-1]
    slab, rank = c_slab.shape
    chunks, block_spec, whole = block_specs(slots, size, rank, slab)
    return pl.pallas_call(
        body,
        grid_spec=pltpu.PrefetchScalarGridSpec(
            num_scalar_prefetch=2,
            grid=(slots, chunks),
            in_specs=[block_spec, whole, whole],
            out_specs=whole,
        ),
        out_shape=jax.ShapeDtypeStruct((slab, rank), F32),
        compiler_params=pltpu.CompilerParams(vmem_limit_bytes=40 * 2**20),
        cost_estimate=pl.CostEstimate(
            flops=2 * slots * size**3 * rank, bytes_accessed=2 * blocks.size, transcendentals=0
        ),
        name=name,
    )(count, coords, blocks, factor, c_slab)


def local(blocks, coords, counts, b_factor, c_factor):
    blocks, coords, count = blocks[0, 0, 0], coords[0, 0, 0], counts[0, 0]
    ia, j, k = (lax.axis_index(name) for name in AXES)
    x, half, core = ia // (NH * NC), ia // NC % NH, ia % NC
    first = core == 0
    piece, rank = b_factor.shape[1:]
    slab = piece * NX * NH * NC * NK
    rows_a = slab * NX * NH * NC
    rows_b = slab * NJ
    rows_c = slab * NK

    mine = jnp.where(first, b_factor[0], c_factor[0])
    other = send(jnp.where(first, c_factor[0], b_factor[0]), flip_core)
    pair = jnp.stack([jnp.where(first, mine, other), jnp.where(first, other, mine)])
    got = send(pair, flip_half)
    quad = jnp.stack([jnp.where(half == 0, pair, got), jnp.where(half == 0, got, pair)])
    ring = ring_gather(quad, k_or_j, jnp.where(first, k, j), axis=2)
    own_slab = ring_gather(ring, along_x, x).reshape(slab, rank)
    own_half = own_slab.astype(BF16)
    other_half = send(own_half, flip_core)
    b_slab = jnp.where(first, own_half, other_half)
    c_slab = jnp.where(first, other_half, own_half)

    own_gram = ring_sum(gram_of(own_slab), j_or_k) * jnp.where(first, 1.0 / rows_b, 1.0 / rows_c)
    other_gram = send(own_gram, flip_core)
    gram_c = jnp.where(first, other_gram, own_gram)
    inverse_one = spd_inverse(own_gram * other_gram)

    m_a = mode_update(mode_one_body, count, coords, blocks, b_slab, c_slab, "mode_one")
    quarter = slab // NK
    m_a = ring_scatter(m_a.reshape(NK, quarter, rank), along_k, k)
    m_a = ring_sum(m_a, along_j)
    m_a = ring_gather(m_a, along_k, k).reshape(slab, rank)
    unscaled_a = dot_full(m_a, inverse_one)

    part = gram_of(unscaled_a).reshape(2, rank // 2, rank)
    keep = lax.dynamic_index_in_dim(part, core, 0, keepdims=False)
    give = lax.dynamic_index_in_dim(part, 1 - core, 0, keepdims=False)
    part = keep + send(give, flip_core)
    part = ring_sum(part, along_x)
    part = part + send(part, flip_half)
    other = send(part, flip_core)
    raw_a = jnp.concatenate([jnp.where(first, part, other), jnp.where(first, other, part)])
    raw_a = raw_a / rows_a
    squares_a = jnp.sum(jnp.where(jnp.eye(rank, dtype=bool), raw_a, 0.0), axis=0)
    scale_a = jnp.sqrt(squares_a + 1e-06)
    own_rows = slab // (NJ * NK)
    a_new = lax.dynamic_slice_in_dim(unscaled_a, (j * NK + k) * own_rows, own_rows, 0) / scale_a
    gram_a = raw_a / (scale_a[:, None] * scale_a[None, :])
    inverse_two = spd_inverse(gram_a * gram_c)

    m_b = mode_update(mode_two_body, count, coords, blocks, unscaled_a.astype(BF16), c_slab, "mode_two")
    m_b = jnp.moveaxis(m_b.reshape(NX * NH, NC, NK, piece, rank), (1, 2), (0, 1))
    keep = lax.dynamic_index_in_dim(m_b, core, 0, keepdims=False)
    give = lax.dynamic_index_in_dim(m_b, 1 - core, 0, keepdims=False)
    m_b = keep + send(give, flip_core)
    m_b = ring_scatter(m_b, along_k, k)
    m_b = m_b + send(m_b, flip_half)
    m_b = ring_sum(m_b, along_x)
    m_b = m_b.reshape(NX * NH * piece, rank) / scale_a
    unscaled_b = dot_full(m_b, inverse_two)
    squares_b = jnp.sum(unscaled_b * unscaled_b, axis=0, keepdims=True)
    squares_b = squares_b + send(squares_b, flip_core)
    squares_b = ring_sum(squares_b, along_k)
    squares_b = ring_sum(squares_b, along_j)
    b_new = lax.dynamic_slice_in_dim(unscaled_b, (x * NH + half) * piece, piece, 0)
    b_new = b_new / jnp.sqrt(squares_b / rows_b + 1e-06)
    return (a_new[None], b_new[None])


def solution(mesh):
    return jax.shard_map(
        local,
        mesh=mesh,
        in_specs=(
            P("ia", "ja", "ka", None, None, None, None),
            P("ia", "ja", "ka", None, None),
            P("ia", "ja", "ka"),
            P("ja", ("ia", "ka"), None),
            P("ka", ("ia", "ja"), None),
        ),
        out_specs=(P("ia", ("ja", "ka"), None), P("ja", ("ia", "ka"), None)),
        check_vma=False,
    )
```

```python
import functools

import jax
import jax.numpy as jnp
from jax import lax
from jax.experimental import pallas as pl
from jax.experimental.pallas import tpu as pltpu
from jax.sharding import PartitionSpec as P

NX, NH, NC, NJ, NK = 4, 2, 2, 4, 4
AXES = ("ia", "ja", "ka")
F32, BF16 = jnp.float32, jnp.bfloat16
CHUNK = 64
EDGE = 64
PANEL = 8
COST_FLOPS = 4 * 10**9
MODE_FLOPS = 12 * 10**9
TOKEN = jax.ShapeDtypeStruct((1, 256), F32)


def flat_index(place):
    x, h, c, j, k = place
    return (((x * NH + h) * NC + c) * NJ + j) * NK + k


PLACES = [
    (x, h, c, j, k)
    for x in range(NX)
    for h in range(NH)
    for c in range(NC)
    for j in range(NJ)
    for k in range(NK)
]


def send(value, move):
    return lax.ppermute(value, AXES, [(flat_index(p), flat_index(move(p))) for p in PLACES])


def flip_core(p):
    return (p[0], p[1], 1 - p[2], p[3], p[4])


def flip_half(p):
    return (p[0], 1 - p[1], p[2], p[3], p[4])


def along_x(s, p):
    return ((p[0] + s) % NX, p[1], p[2], p[3], p[4])


def along_j(s, p):
    return (p[0], p[1], p[2], (p[3] + s) % NJ, p[4])


def along_k(s, p):
    return (p[0], p[1], p[2], p[3], (p[4] + s) % NK)


def k_or_j(s, p):
    return along_k(s, p) if p[2] == 0 else along_j(s, p)


def j_or_k(s, p):
    return along_j(s, p) if p[2] == 0 else along_k(s, p)


def ring_shifts(value, move):
    return [value] + [send(value, functools.partial(move, s)) for s in (1, 2, 3)]


def ring_gather(value, move, me, axis=0):
    got = ring_shifts(value, move)
    return jnp.stack([lax.select_n(lax.rem(me - t + 4, 4), *got) for t in range(4)], axis)


def ring_sum(value, move, dtype=F32):
    got = [g.astype(F32) for g in ring_shifts(value.astype(dtype), move)[1:]]
    return (value + got[0]) + (got[1] + got[2])


def ring_scatter(value, move, me, dtype=F32):
    part = lambda s: lax.dynamic_index_in_dim(value, lax.rem(me + s, 4), 0, keepdims=False)
    got = [send(part(s).astype(dtype), functools.partial(move, s)) for s in (1, 2, 3)]
    got = [g.astype(F32) for g in got]
    return (part(0) + got[0]) + (got[1] + got[2])


def exchange(value, groups):
    return lax.all_to_all(value, AXES, 0, 0, axis_index_groups=groups, tiled=True)


def to_all(value, groups):
    members = len(groups[0])
    got = exchange(jnp.broadcast_to(value[None], (members,) + value.shape), groups)
    return got


def groups_by(key, order):
    found = {}
    for p in PLACES:
        found.setdefault(key(p), []).append(p)
    return [[flat_index(p) for p in sorted(members, key=order)] for members in found.values()]


PLANE_GROUPS = groups_by(lambda p: p[:3], lambda p: p[3:])


def dot_full(a, b):
    return jnp.dot(a, b, precision=lax.Precision.HIGHEST, preferred_element_type=F32)


def gram_of(rows):
    return lax.dot_general(
        rows, rows, (((0,), (0,)), ((), ())),
        precision=lax.Precision.HIGHEST, preferred_element_type=F32,
    )


def small_inverse(d):
    n = d.shape[0]
    lane = lax.broadcasted_iota(jnp.int32, d.shape, 1)
    sub = lax.broadcasted_iota(jnp.int32, d.shape, 0)
    for start in range(0, n, PANEL):
        cols = [jnp.broadcast_to(d[:, start + t : start + t + 1], d.shape) for t in range(PANEL)]
        for t in range(PANEL):
            k = start + t
            col = cols[t]
            pivot = 1.0 / col[k : k + 1, :]
            for u in range(t + 1, PANEL):
                factor = cols[u][k : k + 1, :] * pivot
                cols[u] = jnp.where(sub == k, factor, cols[u] - col * factor)
            row = jnp.where(lane[:1] == k, pivot, d[k : k + 1, :] * pivot)
            d = jnp.where(sub == k, row, jnp.where(lane == k, 0.0, d) - col * row)
    return d


def thirds(x):
    high = x.astype(BF16)
    rest = x - high.astype(F32)
    middle = rest.astype(BF16)
    return high, middle, (rest - middle.astype(F32)).astype(BF16)


def dot_thirds(left, right):
    a, b, c = left
    d, e, f = right
    return jnp.dot(
        jnp.concatenate([a, a, b, b, a, c], axis=1),
        jnp.concatenate([d, e, d, e, f, d], axis=0),
        preferred_element_type=F32,
    )


def eliminate_body(first, last, h_ref, *refs):
    out_ref, token_ref = refs[-2:]
    n = out_ref.shape[0]
    token_ref[...] = jnp.zeros_like(token_ref)
    out_ref[...] = h_ref[...]
    for s in range(first * EDGE, last * EDGE, EDGE):
        block = slice(s, s + EDGE)
        inv = small_inverse(out_ref[block, block])
        panel = thirds(out_ref[:, block])
        out_ref[:, block] = jnp.zeros((n, EDGE), F32)
        out_ref[block, block] = jnp.eye(EDGE, dtype=F32)
        row = dot_thirds(thirds(inv), thirds(out_ref[block, :]))
        out_ref[block, block] = jnp.zeros((EDGE, EDGE), F32)
        out_ref[...] = out_ref[...] - dot_thirds(panel, thirds(row))
        out_ref[block, :] = row


def eliminate(h, first, last, after=()):
    n = h.shape[0]
    steps = last - first
    return pl.pallas_call(
        functools.partial(eliminate_body, first, last),
        out_shape=(jax.ShapeDtypeStruct((n, n), F32), TOKEN),
        in_specs=[pl.BlockSpec(memory_space=pltpu.VMEM)]
        + [pl.BlockSpec(memory_space=pltpu.VMEM)] * len(after),
        out_specs=(pl.BlockSpec(memory_space=pltpu.VMEM),) * 2,
        cost_estimate=pl.CostEstimate(
            flops=steps * COST_FLOPS, bytes_accessed=8 * n * n, transcendentals=0
        ),
        name=f"eliminate_{first}_{last}",
    )(h, *after)


def mode_body(mode, count, coords, x_hbm, factor_ref, c_ref, _, out_ref, token_ref, x_ref, sems):
    slots, size = x_ref.shape[0], x_ref.shape[-1]
    rank = c_ref.shape[-1]
    pieces = size // CHUNK

    def fetch(n, d):
        rows = pl.ds(d * CHUNK, CHUNK)
        return pltpu.make_async_copy(x_hbm.at[n, rows], x_ref.at[n, rows], sems.at[n, d])

    for n in range(slots):

        @pl.when(n < count[0])
        def _():
            for d in range(pieces):
                fetch(n, d).start()

    out_ref[...] = jnp.zeros_like(out_ref)
    token_ref[...] = jnp.zeros_like(token_ref)

    @pl.loop(0, count[0])
    def _(n):
        a_start = pl.multiple_of(coords[n, 0] * size, size)
        b_start = pl.multiple_of(coords[n, 1] * size, size)
        c_rows = c_ref[pl.ds(pl.multiple_of(coords[n, 2] * size, size), size), :]
        if mode == 1:
            b_rows = factor_ref[pl.ds(b_start, size), :].astype(F32)
        else:
            c_wide = c_rows.astype(F32)

        @pl.loop(0, pieces)
        def _(d):
            fetch(n, d).wait()
            start = pl.multiple_of(d * CHUNK, CHUNK)
            rows = pl.ds(pl.multiple_of(a_start + start, CHUNK), CHUNK)
            if mode == 1:
                x = x_ref[n, pl.ds(start, CHUNK)].reshape(CHUNK * size, size)
                prod = jnp.dot(x, c_rows, preferred_element_type=F32)
                part = jnp.sum(prod.reshape(CHUNK, size, rank) * b_rows[None], axis=1)
                out_ref[rows, :] += part
            else:
                a_rows = factor_ref[rows, :].astype(F32)
                left = jnp.concatenate([x_ref[n, start + i] for i in range(CHUNK)], axis=1)
                right = jnp.concatenate(
                    [(c_wide * a_rows[i : i + 1, :]).astype(BF16) for i in range(CHUNK)], axis=0
                )
                out_ref[pl.ds(b_start, size), :] += jnp.dot(
                    left, right, preferred_element_type=F32
                )


def mode_update(mode, count, coords, blocks, factor, c_slab, after):
    slots, size = blocks.shape[0], blocks.shape[-1]
    slab, rank = c_slab.shape
    vmem = pl.BlockSpec(memory_space=pltpu.VMEM)
    smem = pl.BlockSpec(memory_space=pltpu.SMEM)
    anywhere = pl.BlockSpec(memory_space=pl.ANY)
    return pl.pallas_call(
        functools.partial(mode_body, mode),
        in_specs=[smem, smem, anywhere, vmem, vmem, vmem],
        out_specs=(vmem, vmem),
        out_shape=(jax.ShapeDtypeStruct((slab, rank), F32), TOKEN),
        scratch_shapes=[
            pltpu.VMEM(blocks.shape, BF16),
            pltpu.SemaphoreType.DMA((slots, size // CHUNK)),
        ],
        compiler_params=pltpu.CompilerParams(vmem_limit_bytes=56 * 2**20),
        cost_estimate=pl.CostEstimate(
            flops=MODE_FLOPS, bytes_accessed=2 * blocks.size, transcendentals=0
        ),
        name=f"mode_{mode}",
    )(count, coords, blocks, factor, c_slab, after)


def local(blocks, coords, counts, b_factor, c_factor):
    blocks, coords, count = blocks[0, 0, 0], coords[0, 0, 0], counts[0, 0]
    ia, j, k = (lax.axis_index(name) for name in AXES)
    x, half, core = ia // (NH * NC), ia // NC % NH, ia % NC
    first = core == 0
    piece, rank = b_factor.shape[1:]
    slab = piece * NX * NH * NC * NK
    rows_a = slab * NX * NH * NC
    rows_b = slab * NJ
    rows_c = slab * NK

    mine = jnp.where(first, b_factor[0], c_factor[0])
    other = send(jnp.where(first, c_factor[0], b_factor[0]), flip_core)
    pair = jnp.stack([jnp.where(first, mine, other), jnp.where(first, other, mine)])
    got = send(pair, flip_half)
    quad = jnp.stack([jnp.where(half == 0, pair, got), jnp.where(half == 0, got, pair)])
    ring = ring_gather(quad, k_or_j, jnp.where(first, k, j), axis=2)
    own_slab = ring_gather(ring, along_x, x).reshape(slab, rank)
    own_half = own_slab.astype(BF16)
    other_half = send(own_half, flip_core)
    b_slab = jnp.where(first, own_half, other_half)
    c_slab = jnp.where(first, other_half, own_half)

    gram_part = gram_of(own_slab)
    m_a, token = mode_update(1, count, coords, blocks, b_slab, c_slab, gram_part)
    own_gram = ring_sum(gram_part, j_or_k) + token
    own_gram = own_gram * jnp.where(first, 1.0 / rows_b, 1.0 / rows_c)
    other_gram = send(own_gram, flip_core)
    gram_c = jnp.where(first, other_gram, own_gram)

    half_way, token = eliminate(own_gram * other_gram, 0, 2)
    m_a = ring_scatter(m_a.reshape(NK, slab // NK, rank), along_k, k, BF16) + token
    inverse_one, token = eliminate(half_way, 2, 4, (m_a,))
    m_a = ring_sum(m_a, along_j, BF16) + token
    m_a = ring_gather(m_a, along_k, k).reshape(slab, rank)
    own_rows = slab // (NJ * NK)
    unscaled_a = dot_full(m_a, inverse_one)

    part = gram_of(unscaled_a).reshape(2, rank // 2, rank)
    keep = lax.dynamic_index_in_dim(part, core, 0, keepdims=False)
    give = lax.dynamic_index_in_dim(part, 1 - core, 0, keepdims=False)
    part = keep + send(give, flip_core)
    m_b, _ = mode_update(2, count, coords, blocks, unscaled_a.astype(BF16), c_slab, part)
    part = ring_sum(part, along_x)
    m_b = jnp.moveaxis(m_b.reshape(NX * NH, NC, NK, piece, rank), (1, 2), (0, 1))
    keep = lax.dynamic_index_in_dim(m_b, core, 0, keepdims=False)
    give = lax.dynamic_index_in_dim(m_b, 1 - core, 0, keepdims=False)
    part = part + send(part, flip_half)
    m_b = keep + send(give, flip_core)
    m_b = ring_scatter(m_b, along_k, k)
    other = send(part, flip_core)
    raw_a = jnp.concatenate([jnp.where(first, part, other), jnp.where(first, other, part)])
    raw_a = raw_a / rows_a
    squares_a = jnp.sum(jnp.where(jnp.eye(rank, dtype=bool), raw_a, 0.0), axis=0)
    scale_a = jnp.sqrt(squares_a + 1e-06)
    a_new = lax.dynamic_slice_in_dim(unscaled_a, (j * NK + k) * own_rows, own_rows, 0) / scale_a
    gram_a = raw_a / (scale_a[:, None] * scale_a[None, :])
    half_way, token = eliminate(gram_a * gram_c, 0, 2, (m_b,))
    m_b = m_b + send(m_b, flip_half) + token
    inverse_two, _ = eliminate(half_way, 2, 4, (m_b,))
    m_b = ring_sum(m_b, along_x)
    m_b = m_b.reshape(NX * NH * piece, rank) / scale_a
    unscaled_b = dot_full(m_b, inverse_two)
    squares_b = jnp.sum(unscaled_b * unscaled_b, axis=0, keepdims=True)
    squares_b = squares_b + send(squares_b, flip_core)
    squares_b = jnp.sum(to_all(squares_b, PLANE_GROUPS), axis=0)
    b_new = lax.dynamic_slice_in_dim(unscaled_b, (x * NH + half) * piece, piece, 0)
    b_new = b_new / jnp.sqrt(squares_b / rows_b + 1e-06)
    return (a_new[None], b_new[None])


def solution(mesh):
    return jax.shard_map(
        local,
        mesh=mesh,
        in_specs=(
            P("ia", "ja", "ka", None, None, None, None),
            P("ia", "ja", "ka", None, None),
            P("ia", "ja", "ka"),
            P("ja", ("ia", "ka"), None),
            P("ka", ("ia", "ja"), None),
        ),
        out_specs=(P("ia", ("ja", "ka"), None), P("ja", ("ia", "ka"), None)),
        check_vma=False,
    )
```

```python
import functools

import jax
import jax.numpy as jnp
from jax import lax
from jax.experimental import pallas as pl
from jax.experimental.pallas import tpu as pltpu
from jax.sharding import PartitionSpec as P

NX, NH, NC, NJ, NK = 4, 2, 2, 4, 4
AXES = ("ia", "ja", "ka")
F32, BF16 = jnp.float32, jnp.bfloat16
CHUNK = 64
EDGE = 32
PANEL = 16
COST_FLOPS = 2 * 10**9
MODE_FLOPS = 12 * 10**9
TOKEN = jax.ShapeDtypeStruct((1, 256), F32)


def flat_index(place):
    x, h, c, j, k = place
    return (((x * NH + h) * NC + c) * NJ + j) * NK + k


PLACES = [
    (x, h, c, j, k)
    for x in range(NX)
    for h in range(NH)
    for c in range(NC)
    for j in range(NJ)
    for k in range(NK)
]


def send(value, move):
    return lax.ppermute(value, AXES, [(flat_index(p), flat_index(move(p))) for p in PLACES])


def flip_core(p):
    return (p[0], p[1], 1 - p[2], p[3], p[4])


def flip_half(p):
    return (p[0], 1 - p[1], p[2], p[3], p[4])


def along_x(s, p):
    return ((p[0] + s) % NX, p[1], p[2], p[3], p[4])


def along_j(s, p):
    return (p[0], p[1], p[2], (p[3] + s) % NJ, p[4])


def along_k(s, p):
    return (p[0], p[1], p[2], p[3], (p[4] + s) % NK)


def k_or_j(s, p):
    return along_k(s, p) if p[2] == 0 else along_j(s, p)


def j_or_k(s, p):
    return along_j(s, p) if p[2] == 0 else along_k(s, p)


def ring_shifts(value, move):
    return [value] + [send(value, functools.partial(move, s)) for s in (1, 2, 3)]


def ring_gather(value, move, me, axis=0):
    got = ring_shifts(value, move)
    return jnp.stack([lax.select_n(lax.rem(me - t + 4, 4), *got) for t in range(4)], axis)


def ring_sum(value, move, dtype=F32):
    got = [g.astype(F32) for g in ring_shifts(value.astype(dtype), move)[1:]]
    return (value + got[0]) + (got[1] + got[2])


def ring_scatter(value, move, me, dtype=F32):
    part = lambda s: lax.dynamic_index_in_dim(value, lax.rem(me + s, 4), 0, keepdims=False)
    got = [send(part(s).astype(dtype), functools.partial(move, s)) for s in (1, 2, 3)]
    got = [g.astype(F32) for g in got]
    return (part(0) + got[0]) + (got[1] + got[2])


def exchange(value, groups):
    return lax.all_to_all(value, AXES, 0, 0, axis_index_groups=groups, tiled=True)


def to_all(value, groups):
    members = len(groups[0])
    got = exchange(jnp.broadcast_to(value[None], (members,) + value.shape), groups)
    return got


def groups_by(key, order):
    found = {}
    for p in PLACES:
        found.setdefault(key(p), []).append(p)
    return [[flat_index(p) for p in sorted(members, key=order)] for members in found.values()]


PLANE_GROUPS = groups_by(lambda p: p[:3], lambda p: p[3:])
COLUMN_GROUPS = groups_by(lambda p: p[2:], lambda p: p[:2])


def dot_full(a, b):
    return jnp.dot(a, b, precision=lax.Precision.HIGHEST, preferred_element_type=F32)


def gram_of(rows):
    return lax.dot_general(
        rows, rows, (((0,), (0,)), ((), ())),
        precision=lax.Precision.HIGHEST, preferred_element_type=F32,
    )


def small_inverse(d):
    n = d.shape[0]
    lane = lax.broadcasted_iota(jnp.int32, d.shape, 1)
    sub = lax.broadcasted_iota(jnp.int32, d.shape, 0)
    for start in range(0, n, PANEL):
        cols = [jnp.broadcast_to(d[:, start + t : start + t + 1], d.shape) for t in range(PANEL)]
        for t in range(PANEL):
            k = start + t
            col = cols[t]
            pivot = 1.0 / col[k : k + 1, :]
            for u in range(t + 1, PANEL):
                factor = cols[u][k : k + 1, :] * pivot
                cols[u] = jnp.where(sub == k, factor, cols[u] - col * factor)
            row = jnp.where(lane[:1] == k, pivot, d[k : k + 1, :] * pivot)
            d = jnp.where(sub == k, row, jnp.where(lane == k, 0.0, d) - col * row)
    return d


def half_gram_body(x_ref, out_ref):
    x = x_ref[...]
    out_ref[...] = lax.dot_general(x, x, (((0,), (0,)), ((), ())), preferred_element_type=F32)


def half_gram(x):
    vmem = pl.BlockSpec(memory_space=pltpu.VMEM)
    return pl.pallas_call(
        half_gram_body,
        out_shape=jax.ShapeDtypeStruct((x.shape[1],) * 2, F32),
        in_specs=[vmem],
        out_specs=vmem,
        name="half_gram",
    )(x)


def thirds(x):
    high = x.astype(BF16)
    rest = x - high.astype(F32)
    middle = rest.astype(BF16)
    return high, middle, (rest - middle.astype(F32)).astype(BF16)


def dot_thirds(left, right):
    a, b, c = left
    d, e, f = right
    return jnp.dot(
        jnp.concatenate([a, a, b, b, a, c], axis=1),
        jnp.concatenate([d, e, d, e, f, d], axis=0),
        preferred_element_type=F32,
    )


def eliminate_body(first, last, h_ref, *refs):
    out_ref, token_ref = refs[-2:]
    n = out_ref.shape[0]
    token_ref[...] = jnp.zeros_like(token_ref)
    out_ref[...] = h_ref[...]
    for s in range(first * EDGE, last * EDGE, EDGE):
        block = slice(s, s + EDGE)
        inv = small_inverse(out_ref[block, block])
        panel = thirds(out_ref[:, block])
        out_ref[:, block] = jnp.zeros((n, EDGE), F32)
        out_ref[block, block] = jnp.eye(EDGE, dtype=F32)
        row = dot_thirds(thirds(inv), thirds(out_ref[block, :]))
        out_ref[block, block] = jnp.zeros((EDGE, EDGE), F32)
        out_ref[...] = out_ref[...] - dot_thirds(panel, thirds(row))
        out_ref[block, :] = row


def eliminate(h, first, last, after=()):
    n = h.shape[0]
    steps = last - first
    return pl.pallas_call(
        functools.partial(eliminate_body, first, last),
        out_shape=(jax.ShapeDtypeStruct((n, n), F32), TOKEN),
        in_specs=[pl.BlockSpec(memory_space=pltpu.VMEM)]
        + [pl.BlockSpec(memory_space=pltpu.VMEM)] * len(after),
        out_specs=(pl.BlockSpec(memory_space=pltpu.VMEM),) * 2,
        cost_estimate=pl.CostEstimate(
            flops=steps * COST_FLOPS, bytes_accessed=8 * n * n, transcendentals=0
        ),
        name=f"eliminate_{first}_{last}",
    )(h, *after)


def mode_body(mode, meta, x_hbm, factor_ref, c_ref, _, *refs):
    x_ref, total, sems = refs[-3:]
    slots, size = x_ref.shape[0], x_ref.shape[-1]
    rank = c_ref.shape[-1]
    pieces = size // CHUNK
    count = meta[0]

    def fetch(n, d):
        rows = pl.ds(d * CHUNK, CHUNK)
        return pltpu.make_async_copy(x_hbm.at[n, rows], x_ref.at[n, rows], sems.at[n, d])

    for n in range(slots):

        @pl.when(n < count)
        def _():
            for d in range(pieces):
                fetch(n, d).start()

    total[...] = jnp.zeros_like(total)

    @pl.loop(0, count)
    def _(n):
        a_start, b_start, c_start = (
            pl.multiple_of(meta[2 + 3 * n + mode_index] * size, size) for mode_index in range(3)
        )
        c_rows = c_ref[pl.ds(c_start, size), :]
        if mode == 1:
            b_rows = factor_ref[pl.ds(b_start, size), :].astype(F32)
        else:
            c_wide = c_rows.astype(F32)

        @pl.loop(0, pieces)
        def _(d):
            fetch(n, d).wait()
            start = pl.multiple_of(d * CHUNK, CHUNK)
            rows = pl.ds(pl.multiple_of(a_start + start, CHUNK), CHUNK)
            if mode == 1:
                x = x_ref[n, pl.ds(start, CHUNK)].reshape(CHUNK * size, size)
                prod = jnp.dot(x, c_rows, preferred_element_type=F32)
                part = jnp.sum(prod.reshape(CHUNK, size, rank) * b_rows[None], axis=1)
                total[rows, :] += part
            else:
                a_rows = factor_ref[rows, :].astype(F32)
                left = jnp.concatenate([x_ref[n, start + i] for i in range(CHUNK)], axis=1)
                right = jnp.concatenate(
                    [(c_wide * a_rows[i : i + 1, :]).astype(BF16) for i in range(CHUNK)], axis=0
                )
                total[pl.ds(b_start, size), :] += jnp.dot(left, right, preferred_element_type=F32)

    if mode == 1:
        token_ref = refs[4]
        token_ref[...] = jnp.zeros_like(token_ref)
        edge = refs[0].shape[0]
        for shift, ref in enumerate(refs[:4]):
            start = pl.multiple_of(lax.rem(meta[1] + shift, 4) * edge, edge)
            ref[...] = total[pl.ds(start, edge), :].astype(ref.dtype)
    else:
        piece = refs[0].shape[2]
        for ref, core in ((refs[0], meta[1]), (refs[1], 1 - meta[1])):
            for k in range(NK):
                for xh in range(NX * NH):
                    start = ((xh * NC + core) * NK + k) * piece
                    ref[k, xh] = total[pl.ds(pl.multiple_of(start, piece), piece), :].astype(ref.dtype)


def mode_update(mode, meta, blocks, factor, c_slab, after):
    slots, size = blocks.shape[0], blocks.shape[-1]
    slab, rank = c_slab.shape
    vmem = pl.BlockSpec(memory_space=pltpu.VMEM)
    anywhere = pl.BlockSpec(memory_space=pl.ANY)
    if mode == 1:
        rows = (slab // NJ, rank)
        outs = [jax.ShapeDtypeStruct(rows, F32)] + [jax.ShapeDtypeStruct(rows, BF16)] * 3 + [TOKEN]
    else:
        rows = (NK, NX * NH, slab // (NK * NX * NH * NC), rank)
        outs = [jax.ShapeDtypeStruct(rows, F32), jax.ShapeDtypeStruct(rows, BF16)]
    return pl.pallas_call(
        functools.partial(mode_body, mode),
        in_specs=[pl.BlockSpec(memory_space=pltpu.SMEM), anywhere, vmem, vmem, vmem],
        out_specs=[vmem] * len(outs),
        out_shape=outs,
        scratch_shapes=[
            pltpu.VMEM(blocks.shape, BF16),
            pltpu.VMEM((slab, rank), F32),
            pltpu.SemaphoreType.DMA((slots, size // CHUNK)),
        ],
        compiler_params=pltpu.CompilerParams(vmem_limit_bytes=56 * 2**20),
        cost_estimate=pl.CostEstimate(
            flops=MODE_FLOPS, bytes_accessed=2 * blocks.size, transcendentals=0
        ),
        name=f"mode_{mode}",
    )(meta, blocks, factor, c_slab, after)


def local(blocks, coords, counts, b_factor, c_factor):
    blocks = blocks[0, 0, 0]
    ia, j, k = (lax.axis_index(name) for name in AXES)
    x, half, core = ia // (NH * NC), ia // NC % NH, ia % NC
    first = core == 0
    piece, rank = b_factor.shape[1:]
    slab = piece * NX * NH * NC * NK
    rows_a = slab * NX * NH * NC
    rows_b = slab * NJ
    rows_c = slab * NK

    mine = jnp.where(first, b_factor[0], c_factor[0])
    other = send(jnp.where(first, c_factor[0], b_factor[0]), flip_core)
    pair = jnp.stack([jnp.where(first, mine, other), jnp.where(first, other, mine)])
    got = send(pair, flip_half)
    meta = jnp.concatenate([counts.reshape(-1), j[None], coords.reshape(-1)])
    meta_two = jnp.concatenate([counts.reshape(-1), core[None], coords.reshape(-1)])
    ready = jnp.minimum(jnp.min(meta), 0) + jnp.minimum(jnp.min(meta_two), 0)
    quad = jnp.stack([jnp.where(half == 0, pair, got), jnp.where(half == 0, got, pair)])
    quad = quad + ready.astype(F32)
    ring = ring_gather(quad, k_or_j, jnp.where(first, k, j), axis=2)
    own_slab = ring_gather(ring, along_x, x).reshape(slab, rank)
    own_half = own_slab.astype(BF16)
    other_half = send(own_half, flip_core)
    b_slab = jnp.where(first, own_half, other_half)
    c_slab = jnp.where(first, other_half, own_half)

    gram_part = gram_of(own_slab)
    kept, *gone, token = mode_update(1, meta, blocks, b_slab, c_slab, gram_part)
    own_gram = ring_sum(gram_part, j_or_k) + token
    own_gram = own_gram * jnp.where(first, 1.0 / rows_b, 1.0 / rows_c)
    other_gram = send(own_gram, flip_core)
    gram_c = jnp.where(first, other_gram, own_gram)

    half_way, token = eliminate(own_gram * other_gram, 0, 4)
    got = [send(g, functools.partial(along_j, i + 1)).astype(F32) for i, g in enumerate(gone)]
    m_a = (kept + got[0]) + (got[1] + got[2]) + token
    inverse_one, token = eliminate(half_way, 4, 8, (m_a,))
    m_a = ring_sum(m_a, along_k, BF16) + token
    unscaled_a = dot_full(m_a, inverse_one)
    a_slab = ring_gather(unscaled_a.astype(BF16), along_j, j).reshape(slab, rank)

    part = half_gram(a_slab).reshape(2, rank // 2, rank)
    keep = lax.dynamic_index_in_dim(part, core, 0, keepdims=False)
    give = lax.dynamic_index_in_dim(part, 1 - core, 0, keepdims=False)
    part = keep + send(give, flip_core)
    keep, give = mode_update(2, meta_two, blocks, a_slab, c_slab, part)
    part = ring_sum(part, along_x)
    part = part + send(part, flip_half)
    m_b = keep + send(give, flip_core).astype(F32)
    m_b = ring_scatter(m_b, along_k, k, BF16)
    other = send(part, flip_core)
    raw_a = jnp.concatenate([jnp.where(first, part, other), jnp.where(first, other, part)])
    inverse_two, _ = eliminate(raw_a * gram_c, 0, 8, (m_b,))
    squares_a = jnp.sum(jnp.where(jnp.eye(rank, dtype=bool), raw_a, 0.0), axis=0)
    scale_a = jnp.sqrt(squares_a / rows_a + 1e-06)
    own_rows = slab // (NJ * NK)
    a_new = lax.dynamic_slice_in_dim(unscaled_a, k * own_rows, own_rows, 0) / scale_a
    m_b = jnp.sum(to_all(m_b.astype(BF16), COLUMN_GROUPS).astype(F32), axis=0)
    unscaled_b = dot_full(m_b.reshape(NX * NH * piece, rank), inverse_two) * (rows_a * scale_a)
    squares_b = jnp.sum(unscaled_b * unscaled_b, axis=0, keepdims=True)
    squares_b = squares_b + send(squares_b, flip_core)
    squares_b = jnp.sum(to_all(squares_b, PLANE_GROUPS), axis=0)
    b_new = lax.dynamic_slice_in_dim(unscaled_b, (x * NH + half) * piece, piece, 0)
    b_new = b_new / jnp.sqrt(squares_b / rows_b + 1e-06)
    return (a_new[None], b_new[None])


def solution(mesh):
    return jax.shard_map(
        local,
        mesh=mesh,
        in_specs=(
            P("ia", "ja", "ka", None, None, None, None),
            P("ia", "ja", "ka", None, None),
            P("ia", "ja", "ka"),
            P("ja", ("ia", "ka"), None),
            P("ka", ("ia", "ja"), None),
        ),
        out_specs=(P("ia", ("ja", "ka"), None), P("ja", ("ia", "ka"), None)),
        check_vma=False,
    )
```

```python
import functools

import jax
import jax.numpy as jnp
from jax import lax
from jax.experimental import pallas as pl
from jax.experimental.pallas import tpu as pltpu
from jax.sharding import PartitionSpec as P

NX, NH, NC, NJ, NK = 4, 2, 2, 4, 4
AXES = ("ia", "ja", "ka")
F32, BF16 = jnp.float32, jnp.bfloat16
CHUNK = 64
EDGE = 32
PANEL = 16
J_AT, CORE_AT = 10, 11
COST_FLOPS = 2 * 10**9
MODE_FLOPS = 12 * 10**9
TOKEN = jax.ShapeDtypeStruct((1, 256), F32)


def flat_index(place):
    x, h, c, j, k = place
    return (((x * NH + h) * NC + c) * NJ + j) * NK + k


PLACES = [
    (x, h, c, j, k)
    for x in range(NX)
    for h in range(NH)
    for c in range(NC)
    for j in range(NJ)
    for k in range(NK)
]


def send(value, move):
    return lax.ppermute(value, AXES, [(flat_index(p), flat_index(move(p))) for p in PLACES])


def flip_core(p):
    return (p[0], p[1], 1 - p[2], p[3], p[4])


def flip_half(p):
    return (p[0], 1 - p[1], p[2], p[3], p[4])


def along_x(s, p):
    return ((p[0] + s) % NX, p[1], p[2], p[3], p[4])


def along_j(s, p):
    return (p[0], p[1], p[2], (p[3] + s) % NJ, p[4])


def along_k(s, p):
    return (p[0], p[1], p[2], p[3], (p[4] + s) % NK)


def k_or_j(s, p):
    return along_k(s, p) if p[2] == 0 else along_j(s, p)


def j_or_k(s, p):
    return along_j(s, p) if p[2] == 0 else along_k(s, p)


def ring_shifts(value, move):
    return [value] + [send(value, functools.partial(move, s)) for s in (1, 2, 3)]


def ring_gather(value, move, me, axis=0):
    got = ring_shifts(value, move)
    return jnp.stack([lax.select_n(lax.rem(me - t + 4, 4), *got) for t in range(4)], axis)


def ring_sum(value, move, dtype=F32):
    got = [g.astype(F32) for g in ring_shifts(value.astype(dtype), move)[1:]]
    return (value + got[0]) + (got[1] + got[2])


def ring_scatter(value, move, me, dtype=F32):
    part = lambda s: lax.dynamic_index_in_dim(value, lax.rem(me + s, 4), 0, keepdims=False)
    got = [send(part(s).astype(dtype), functools.partial(move, s)) for s in (1, 2, 3)]
    got = [g.astype(F32) for g in got]
    return (part(0) + got[0]) + (got[1] + got[2])


def exchange(value, groups):
    return lax.all_to_all(value, AXES, 0, 0, axis_index_groups=groups, tiled=True)


def to_all(value, groups):
    members = len(groups[0])
    got = exchange(jnp.broadcast_to(value[None], (members,) + value.shape), groups)
    return got


def groups_by(key, order):
    found = {}
    for p in PLACES:
        found.setdefault(key(p), []).append(p)
    return [[flat_index(p) for p in sorted(members, key=order)] for members in found.values()]


PLANE_GROUPS = groups_by(lambda p: p[:3], lambda p: p[3:])
COLUMN_GROUPS = groups_by(lambda p: p[2:], lambda p: p[:2])


def dot_full(a, b):
    return jnp.dot(a, b, precision=lax.Precision.HIGHEST, preferred_element_type=F32)


def gram_of(rows):
    return lax.dot_general(
        rows, rows, (((0,), (0,)), ((), ())),
        precision=lax.Precision.HIGHEST, preferred_element_type=F32,
    )


def small_inverse(d):
    n = d.shape[0]
    lane = lax.broadcasted_iota(jnp.int32, d.shape, 1)
    sub = lax.broadcasted_iota(jnp.int32, d.shape, 0)
    for start in range(0, n, PANEL):
        cols = [jnp.broadcast_to(d[:, start + t : start + t + 1], d.shape) for t in range(PANEL)]
        for t in range(PANEL):
            k = start + t
            col = cols[t]
            pivot = 1.0 / col[k : k + 1, :]
            for u in range(t + 1, PANEL):
                factor = cols[u][k : k + 1, :] * pivot
                cols[u] = jnp.where(sub == k, factor, cols[u] - col * factor)
            row = jnp.where(lane[:1] == k, pivot, d[k : k + 1, :] * pivot)
            d = jnp.where(sub == k, row, jnp.where(lane == k, 0.0, d) - col * row)
    return d


def thirds(x):
    high = x.astype(BF16)
    rest = x - high.astype(F32)
    middle = rest.astype(BF16)
    return high, middle, (rest - middle.astype(F32)).astype(BF16)


def dot_thirds(left, right):
    a, b, c = left
    d, e, f = right
    return jnp.dot(
        jnp.concatenate([a, a, b, b, a, c], axis=1),
        jnp.concatenate([d, e, d, e, f, d], axis=0),
        preferred_element_type=F32,
    )


def eliminate_body(kind, rows, first, last, *refs):
    out_ref, row_ref, token_ref = refs[-3:]
    n = out_ref.shape[0]
    token_ref[...] = jnp.zeros_like(token_ref)
    if kind == "halves":
        core, near_ref, far_ref, factor_ref = refs[:4]
        for ref, place in ((near_ref, core[CORE_AT]), (far_ref, 1 - core[CORE_AT])):
            out_ref[pl.ds(pl.multiple_of(place * (n // 2), n // 2), n // 2), :] = ref[...]
        diagonal = lax.broadcasted_iota(jnp.int32, (n, n), 0) == lax.broadcasted_iota(
            jnp.int32, (n, n), 1
        )
        squares = jnp.sum(jnp.where(diagonal, out_ref[...], 0.0), axis=0, keepdims=True)
        row_ref[...] = jnp.sqrt(squares / rows + 1e-06)
        out_ref[...] = out_ref[...] * factor_ref[...]
    elif kind == "product":
        row_ref[...] = jnp.zeros_like(row_ref)
        out_ref[...] = refs[0][...] * refs[1][...]
    else:
        row_ref[...] = jnp.zeros_like(row_ref)
        out_ref[...] = refs[0][...]
    for s in range(first * EDGE, last * EDGE, EDGE):
        block = slice(s, s + EDGE)
        inv = small_inverse(out_ref[block, block])
        panel = thirds(out_ref[:, block])
        out_ref[:, block] = jnp.zeros((n, EDGE), F32)
        out_ref[block, block] = jnp.eye(EDGE, dtype=F32)
        row = dot_thirds(thirds(inv), thirds(out_ref[block, :]))
        out_ref[block, block] = jnp.zeros((EDGE, EDGE), F32)
        out_ref[...] = out_ref[...] - dot_thirds(panel, thirds(row))
        out_ref[block, :] = row


def eliminate(kind, given, first, last, after=(), rows=1):
    n = given[-1].shape[-1]
    steps = last - first
    vmem = pl.BlockSpec(memory_space=pltpu.VMEM)
    places = [vmem] * len(given) + [pl.BlockSpec(memory_space=pl.ANY)] * len(after)
    if kind == "halves":
        places[0] = pl.BlockSpec(memory_space=pltpu.SMEM)
    return pl.pallas_call(
        functools.partial(eliminate_body, kind, rows, first, last),
        out_shape=(jax.ShapeDtypeStruct((n, n), F32), TOKEN, TOKEN),
        in_specs=places,
        out_specs=(vmem,) * 3,
        cost_estimate=pl.CostEstimate(
            flops=steps * COST_FLOPS, bytes_accessed=8 * n * n, transcendentals=0
        ),
        name=f"eliminate_{first}_{last}",
    )(*given, *after)


def assemble_body(place, a_ref, b_ref, c_ref, d_ref, slab_ref, near_ref, far_ref, gram_ref):
    edge = a_ref.shape[0]
    for shift, ref in enumerate((a_ref, b_ref, c_ref, d_ref)):
        start = pl.multiple_of(lax.rem(place[J_AT] - shift + 4, 4) * edge, edge)
        slab_ref[pl.ds(start, edge), :] = ref[...]
    x = slab_ref[...]
    gram_ref[...] = lax.dot_general(x, x, (((0,), (0,)), ((), ())), preferred_element_type=F32)
    edge = near_ref.shape[0]
    for ref, core in ((near_ref, place[CORE_AT]), (far_ref, 1 - place[CORE_AT])):
        ref[...] = gram_ref[pl.ds(pl.multiple_of(core * edge, edge), edge), :]


def assemble(pieces, meta):
    edge, rank = pieces[0].shape
    vmem = pl.BlockSpec(memory_space=pltpu.VMEM)
    half = jax.ShapeDtypeStruct((rank // 2, rank), F32)
    return pl.pallas_call(
        assemble_body,
        out_shape=[jax.ShapeDtypeStruct((4 * edge, rank), BF16), half, half],
        in_specs=[pl.BlockSpec(memory_space=pltpu.SMEM)] + [vmem] * 4,
        out_specs=[vmem] * 3,
        scratch_shapes=[pltpu.VMEM((rank, rank), F32)],
        name="assemble",
    )(meta, *pieces)


def zero_of(value):
    return jnp.minimum(jnp.abs(value[:1]), 0.0)


def mode_body(mode, meta, x_hbm, head_ref, factor_ref, c_ref, _, *refs):
    x_ref, total, sems = refs[-3:]
    slots, size = x_ref.shape[0], x_ref.shape[-1]
    rank = c_ref.shape[-1]
    pieces = size // CHUNK
    count = meta[0]

    def fetch(n, d):
        rows = pl.ds(d * CHUNK, CHUNK)
        return pltpu.make_async_copy(x_hbm.at[n, rows], x_ref.at[n, rows], sems.at[n, d])

    for n in range(slots):

        @pl.when(n < count)
        def _():
            for d in range(1 if n == 0 else 0, pieces):
                fetch(n, d).start()

    total[...] = jnp.zeros_like(total)

    def step(n, d, x):
        a_start, b_start, c_start = (
            pl.multiple_of(meta[1 + 3 * n + mode_index] * size, size) for mode_index in range(3)
        )
        c_rows = c_ref[pl.ds(c_start, size), :]
        rows = pl.ds(pl.multiple_of(a_start + d * CHUNK, CHUNK), CHUNK)
        if mode == 1:
            b_rows = factor_ref[pl.ds(b_start, size), :].astype(F32)
            prod = jnp.dot(x.reshape(CHUNK * size, size), c_rows, preferred_element_type=F32)
            part = jnp.sum(prod.reshape(CHUNK, size, rank) * b_rows[None], axis=1)
            total[rows, :] += part
        else:
            a_rows = factor_ref[rows, :].astype(F32)
            c_wide = c_rows.astype(F32)
            left = jnp.concatenate([x[i] for i in range(CHUNK)], axis=1)
            right = jnp.concatenate(
                [(c_wide * a_rows[i : i + 1, :]).astype(BF16) for i in range(CHUNK)], axis=0
            )
            total[pl.ds(b_start, size), :] += jnp.dot(left, right, preferred_element_type=F32)

    step(0, 0, head_ref[...])

    @pl.loop(0, count)
    def _(n):
        @pl.loop(jnp.where(n == 0, 1, 0), pieces)
        def _(d):
            fetch(n, d).wait()
            step(n, d, x_ref[n, pl.ds(pl.multiple_of(d * CHUNK, CHUNK), CHUNK)])

    if mode == 1:
        token_ref = refs[4]
        token_ref[...] = jnp.zeros_like(token_ref)
        edge = refs[0].shape[0]
        for shift, ref in enumerate(refs[:4]):
            start = pl.multiple_of(lax.rem(meta[J_AT] + shift, 4) * edge, edge)
            ref[...] = total[pl.ds(start, edge), :].astype(ref.dtype)
    else:
        piece = refs[0].shape[2]
        for ref, core in ((refs[0], meta[CORE_AT]), (refs[1], 1 - meta[CORE_AT])):
            for k in range(NK):
                for xh in range(NX * NH):
                    start = ((xh * NC + core) * NK + k) * piece
                    ref[k, xh] = total[pl.ds(pl.multiple_of(start, piece), piece), :].astype(ref.dtype)


def mode_update(mode, meta, blocks, head, factor, c_slab, after):
    slots, size = blocks.shape[0], blocks.shape[-1]
    slab, rank = c_slab.shape
    vmem = pl.BlockSpec(memory_space=pltpu.VMEM)
    anywhere = pl.BlockSpec(memory_space=pl.ANY)
    if mode == 1:
        rows = (slab // NJ, rank)
        outs = [jax.ShapeDtypeStruct(rows, F32)] + [jax.ShapeDtypeStruct(rows, BF16)] * 3 + [TOKEN]
    else:
        rows = (NK, NX * NH, slab // (NK * NX * NH * NC), rank)
        outs = [jax.ShapeDtypeStruct(rows, F32), jax.ShapeDtypeStruct(rows, BF16)]
    return pl.pallas_call(
        functools.partial(mode_body, mode),
        in_specs=[pl.BlockSpec(memory_space=pltpu.SMEM), anywhere, vmem, vmem, vmem, anywhere],
        out_specs=[vmem] * len(outs),
        out_shape=outs,
        scratch_shapes=[
            pltpu.VMEM(blocks.shape, BF16),
            pltpu.VMEM((slab, rank), F32),
            pltpu.SemaphoreType.DMA((slots, size // CHUNK)),
        ],
        compiler_params=pltpu.CompilerParams(vmem_limit_bytes=48 * 2**20),
        cost_estimate=pl.CostEstimate(
            flops=MODE_FLOPS, bytes_accessed=2 * blocks.size, transcendentals=0
        ),
        name=f"mode_{mode}",
    )(meta, blocks, head, factor, c_slab, after)


def local(blocks, coords, counts, b_factor, c_factor):
    blocks = blocks[0, 0, 0]
    ia, j, k = (lax.axis_index(name) for name in AXES)
    x, half, core = ia // (NH * NC), ia // NC % NH, ia % NC
    first = core == 0
    piece, rank = b_factor.shape[1:]
    slab = piece * NX * NH * NC * NK
    rows_a = slab * NX * NH * NC
    rows_b = slab * NJ
    rows_c = slab * NK

    mine = jnp.where(first, b_factor[0], c_factor[0])
    other = send(jnp.where(first, c_factor[0], b_factor[0]), flip_core)
    pair = jnp.stack([jnp.where(first, mine, other), jnp.where(first, other, mine)])
    got = send(pair, flip_half)
    quad = jnp.stack([jnp.where(half == 0, pair, got), jnp.where(half == 0, got, pair)])
    ring = ring_gather(quad, k_or_j, jnp.where(first, k, j), axis=2)
    own_slab = ring_gather(ring, along_x, x).reshape(slab, rank)
    meta = jnp.concatenate([counts.reshape(-1), coords.reshape(-1), j[None], core[None]])
    meta, head = lax.optimization_barrier((meta, blocks[0, :CHUNK]))
    ready = jnp.minimum(jnp.min(meta), 0).astype(F32) + zero_of(head[0, 0, :1].astype(F32))
    own_half = (own_slab + ready).astype(BF16)
    other_half = send(own_half, flip_core)
    b_slab = jnp.where(first, own_half, other_half)
    c_slab = jnp.where(first, other_half, own_half)

    gram_part = gram_of(own_slab)
    kept, *gone, token = mode_update(1, meta, blocks, head, b_slab, c_slab, gram_part)
    own_gram = ring_sum(gram_part, j_or_k) + token
    own_gram = own_gram * jnp.where(first, 1.0 / rows_b, 1.0 / rows_c)
    other_gram = send(own_gram, flip_core)
    gram_c = jnp.where(first, other_gram, own_gram)

    half_way, _, token = eliminate("product", (own_gram, other_gram), 0, 4)
    got = [send(g, functools.partial(along_j, i + 1)).astype(F32) for i, g in enumerate(gone)]
    m_a = (kept + got[0]) + (got[1] + got[2]) + token
    inverse_one, _, token = eliminate("plain", (half_way,), 4, 8, (m_a,))
    m_a = ring_sum(m_a, along_k, BF16) + token
    unscaled_a = dot_full(m_a, inverse_one)

    a_slab, near, far = assemble(ring_shifts(unscaled_a.astype(BF16), along_j), meta)
    part = near + send(far, flip_core)
    keep, give = mode_update(2, meta, blocks, head, a_slab, c_slab, part)
    part = ring_sum(part, along_x)
    m_b = keep + send(give, flip_core).astype(F32) + zero_of(part)
    part = part + send(part, flip_half)
    m_b = ring_scatter(m_b, along_k, k, BF16)
    other = send(part, flip_core)
    inverse_two, scale_a, _ = eliminate("halves", (meta, part, other, gram_c), 0, 8, (m_b,), rows_a)
    own_rows = slab // (NJ * NK)
    a_new = lax.dynamic_slice_in_dim(unscaled_a, k * own_rows, own_rows, 0) / scale_a
    m_b = jnp.sum(to_all(m_b.astype(BF16), COLUMN_GROUPS).astype(F32), axis=0)
    unscaled_b = dot_full(m_b.reshape(NX * NH * piece, rank), inverse_two) * (rows_a * scale_a)
    squares_b = jnp.sum(unscaled_b * unscaled_b, axis=0, keepdims=True)
    squares_b = squares_b + send(squares_b, flip_core)
    squares_b = jnp.sum(to_all(squares_b, PLANE_GROUPS), axis=0)
    b_new = lax.dynamic_slice_in_dim(unscaled_b, (x * NH + half) * piece, piece, 0)
    b_new = b_new / jnp.sqrt(squares_b / rows_b + 1e-06)
    return (a_new[None], b_new[None])


def solution(mesh):
    return jax.shard_map(
        local,
        mesh=mesh,
        in_specs=(
            P("ia", "ja", "ka", None, None, None, None),
            P("ia", "ja", "ka", None, None),
            P("ia", "ja", "ka"),
            P("ja", ("ia", "ka"), None),
            P("ka", ("ia", "ja"), None),
        ),
        out_specs=(P("ia", ("ja", "ka"), None), P("ja", ("ia", "ka"), None)),
        check_vma=False,
    )
```

```python
import functools

import jax
import jax.numpy as jnp
from jax import lax
from jax.experimental import pallas as pl
from jax.experimental.pallas import tpu as pltpu
from jax.sharding import PartitionSpec as P

NX, NH, NC, NJ, NK = 4, 2, 2, 4, 4
AXES = ("ia", "ja", "ka")
F32, BF16 = jnp.float32, jnp.bfloat16
CHUNK = 64
EDGE = 32
PANEL = 16
J_AT, CORE_AT = 10, 11
COST_FLOPS = 2 * 10**9
MODE_FLOPS = 12 * 10**9
TOKEN = jax.ShapeDtypeStruct((1, 256), F32)


def flat_index(place):
    x, h, c, j, k = place
    return (((x * NH + h) * NC + c) * NJ + j) * NK + k


PLACES = [
    (x, h, c, j, k)
    for x in range(NX)
    for h in range(NH)
    for c in range(NC)
    for j in range(NJ)
    for k in range(NK)
]


def send(value, move):
    return lax.ppermute(value, AXES, [(flat_index(p), flat_index(move(p))) for p in PLACES])


def flip_core(p):
    return (p[0], p[1], 1 - p[2], p[3], p[4])


def flip_half(p):
    return (p[0], 1 - p[1], p[2], p[3], p[4])


def along_x(s, p):
    return ((p[0] + s) % NX, p[1], p[2], p[3], p[4])


def along_j(s, p):
    return (p[0], p[1], p[2], (p[3] + s) % NJ, p[4])


def along_k(s, p):
    return (p[0], p[1], p[2], p[3], (p[4] + s) % NK)


def k_or_j(s, p):
    return along_k(s, p) if p[2] == 0 else along_j(s, p)


def j_or_k(s, p):
    return along_j(s, p) if p[2] == 0 else along_k(s, p)


def ring_shifts(value, move):
    return [value] + [send(value, functools.partial(move, s)) for s in (1, 2, 3)]


def ring_gather(value, move, me, axis=0):
    got = ring_shifts(value, move)
    return jnp.stack([lax.select_n(lax.rem(me - t + 4, 4), *got) for t in range(4)], axis)


def ring_sum(value, move, dtype=F32):
    got = [g.astype(F32) for g in ring_shifts(value.astype(dtype), move)[1:]]
    return (value + got[0]) + (got[1] + got[2])


def ring_scatter(value, move, me, dtype=F32):
    part = lambda s: lax.dynamic_index_in_dim(value, lax.rem(me + s, 4), 0, keepdims=False)
    got = [send(part(s).astype(dtype), functools.partial(move, s)) for s in (1, 2, 3)]
    got = [g.astype(F32) for g in got]
    return (part(0) + got[0]) + (got[1] + got[2])


def exchange(value, groups):
    return lax.all_to_all(value, AXES, 0, 0, axis_index_groups=groups, tiled=True)


def to_all(value, groups):
    members = len(groups[0])
    got = exchange(jnp.broadcast_to(value[None], (members,) + value.shape), groups)
    return got


def groups_by(key, order):
    found = {}
    for p in PLACES:
        found.setdefault(key(p), []).append(p)
    return [[flat_index(p) for p in sorted(members, key=order)] for members in found.values()]


PLANE_GROUPS = groups_by(lambda p: p[:3], lambda p: p[3:])
COLUMN_GROUPS = groups_by(lambda p: p[2:], lambda p: p[:2])


def dot_full(a, b):
    return jnp.dot(a, b, precision=lax.Precision.HIGHEST, preferred_element_type=F32)


def gram_of(rows):
    return lax.dot_general(
        rows, rows, (((0,), (0,)), ((), ())),
        precision=lax.Precision.HIGHEST, preferred_element_type=F32,
    )


def small_inverse(d):
    n = d.shape[0]
    lane = lax.broadcasted_iota(jnp.int32, d.shape, 1)
    sub = lax.broadcasted_iota(jnp.int32, d.shape, 0)
    for start in range(0, n, PANEL):
        cols = [jnp.broadcast_to(d[:, start + t : start + t + 1], d.shape) for t in range(PANEL)]
        for t in range(PANEL):
            k = start + t
            col = cols[t]
            pivot = 1.0 / col[k : k + 1, :]
            for u in range(t + 1, PANEL):
                factor = cols[u][k : k + 1, :] * pivot
                cols[u] = jnp.where(sub == k, factor, cols[u] - col * factor)
            row = jnp.where(lane[:1] == k, pivot, d[k : k + 1, :] * pivot)
            d = jnp.where(sub == k, row, jnp.where(lane == k, 0.0, d) - col * row)
    return d


def thirds(x):
    high = x.astype(BF16)
    rest = x - high.astype(F32)
    middle = rest.astype(BF16)
    return high, middle, (rest - middle.astype(F32)).astype(BF16)


def dot_thirds(left, right):
    a, b, c = left
    d, e, f = right
    return jnp.dot(
        jnp.concatenate([a, a, b, b, a, c], axis=1),
        jnp.concatenate([d, e, d, e, f, d], axis=0),
        preferred_element_type=F32,
    )


def eliminate_body(kind, rows, first, last, *refs):
    out_ref, row_ref, token_ref = refs[-3:]
    n = out_ref.shape[0]
    token_ref[...] = jnp.zeros_like(token_ref)
    if kind == "halves":
        core, near_ref, far_ref, factor_ref = refs[:4]
        for ref, place in ((near_ref, core[CORE_AT]), (far_ref, 1 - core[CORE_AT])):
            out_ref[pl.ds(pl.multiple_of(place * (n // 2), n // 2), n // 2), :] = ref[...]
        diagonal = lax.broadcasted_iota(jnp.int32, (n, n), 0) == lax.broadcasted_iota(
            jnp.int32, (n, n), 1
        )
        squares = jnp.sum(jnp.where(diagonal, out_ref[...], 0.0), axis=0, keepdims=True)
        row_ref[...] = jnp.sqrt(squares / rows + 1e-06)
        token_ref[...] = rows * row_ref[...]
        out_ref[...] = out_ref[...] * factor_ref[...]
    elif kind == "product":
        row_ref[...] = jnp.zeros_like(row_ref)
        out_ref[...] = refs[0][...] * refs[1][...]
    else:
        row_ref[...] = jnp.zeros_like(row_ref)
        out_ref[...] = refs[0][...]
    for s in range(first * EDGE, last * EDGE, EDGE):
        block = slice(s, s + EDGE)
        inv = small_inverse(out_ref[block, block])
        panel = thirds(out_ref[:, block])
        out_ref[:, block] = jnp.zeros((n, EDGE), F32)
        out_ref[block, block] = jnp.eye(EDGE, dtype=F32)
        row = dot_thirds(thirds(inv), thirds(out_ref[block, :]))
        out_ref[block, block] = jnp.zeros((EDGE, EDGE), F32)
        out_ref[...] = out_ref[...] - dot_thirds(panel, thirds(row))
        out_ref[block, :] = row


def eliminate(kind, given, first, last, after=(), rows=1):
    n = given[-1].shape[-1]
    steps = last - first
    vmem = pl.BlockSpec(memory_space=pltpu.VMEM)
    places = [vmem] * len(given) + [pl.BlockSpec(memory_space=pl.ANY)] * len(after)
    if kind == "halves":
        places[0] = pl.BlockSpec(memory_space=pltpu.SMEM)
    return pl.pallas_call(
        functools.partial(eliminate_body, kind, rows, first, last),
        out_shape=(jax.ShapeDtypeStruct((n, n), F32), TOKEN, TOKEN),
        in_specs=places,
        out_specs=(vmem,) * 3,
        cost_estimate=pl.CostEstimate(
            flops=steps * COST_FLOPS, bytes_accessed=8 * n * n, transcendentals=0
        ),
        name=f"eliminate_{first}_{last}",
    )(*given, *after)


def assemble_body(place, a_ref, b_ref, c_ref, d_ref, slab_ref, near_ref, far_ref, gram_ref):
    edge = a_ref.shape[0]
    for shift, ref in enumerate((a_ref, b_ref, c_ref, d_ref)):
        start = pl.multiple_of(lax.rem(place[J_AT] - shift + 4, 4) * edge, edge)
        slab_ref[pl.ds(start, edge), :] = ref[...]
    x = slab_ref[...]
    gram_ref[...] = lax.dot_general(x, x, (((0,), (0,)), ((), ())), preferred_element_type=F32)
    edge = near_ref.shape[0]
    for ref, core in ((near_ref, place[CORE_AT]), (far_ref, 1 - place[CORE_AT])):
        ref[...] = gram_ref[pl.ds(pl.multiple_of(core * edge, edge), edge), :]


def assemble(pieces, meta):
    edge, rank = pieces[0].shape
    vmem = pl.BlockSpec(memory_space=pltpu.VMEM)
    half = jax.ShapeDtypeStruct((rank // 2, rank), F32)
    return pl.pallas_call(
        assemble_body,
        out_shape=[jax.ShapeDtypeStruct((4 * edge, rank), BF16), half, half],
        in_specs=[pl.BlockSpec(memory_space=pltpu.SMEM)] + [vmem] * 4,
        out_specs=[vmem] * 3,
        scratch_shapes=[pltpu.VMEM((rank, rank), F32)],
        name="assemble",
    )(meta, *pieces)


def zero_of(value):
    return jnp.minimum(jnp.abs(value[:1]), 0.0)


def mode_body(mode, meta, x_hbm, head_ref, a_ref, own_ref, other_ref, _, *refs):
    x_ref, total, sems = refs[-3:]
    slots, size = x_ref.shape[0], x_ref.shape[-1]
    rank = own_ref.shape[-1]
    pieces = size // CHUNK
    count = meta[0]

    def fetch(n, d):
        rows = pl.ds(d * CHUNK, CHUNK)
        return pltpu.make_async_copy(x_hbm.at[n, rows], x_ref.at[n, rows], sems.at[n, d])

    for n in range(slots):

        @pl.when(n < count)
        def _():
            for d in range(1 if n == 0 else 0, pieces):
                fetch(n, d).start()

    total[...] = jnp.zeros_like(total)

    def step(n, d, x):
        a_start, b_start, c_start = (
            pl.multiple_of(meta[1 + 3 * n + mode_index] * size, size) for mode_index in range(3)
        )
        first = meta[CORE_AT] == 0
        c_rows = pl.ds(c_start, size)
        c_wide = jnp.where(
            first, other_ref[c_rows, :].astype(F32), own_ref[c_rows, :].astype(F32)
        )
        rows = pl.ds(pl.multiple_of(a_start + d * CHUNK, CHUNK), CHUNK)
        if mode == 1:
            b_rows = pl.ds(b_start, size)
            b_rows = jnp.where(
                first, own_ref[b_rows, :].astype(F32), other_ref[b_rows, :].astype(F32)
            )
            c_half = c_wide.astype(BF16)
            prod = jnp.dot(x.reshape(CHUNK * size, size), c_half, preferred_element_type=F32)
            part = jnp.sum(prod.reshape(CHUNK, size, rank) * b_rows[None], axis=1)
            total[rows, :] += part
        else:
            a_rows = a_ref[rows, :].astype(F32)
            left = jnp.concatenate([x[i] for i in range(CHUNK)], axis=1)
            right = jnp.concatenate(
                [(c_wide * a_rows[i : i + 1, :]).astype(BF16) for i in range(CHUNK)], axis=0
            )
            total[pl.ds(b_start, size), :] += jnp.dot(left, right, preferred_element_type=F32)

    step(0, 0, head_ref[...])

    @pl.loop(0, count)
    def _(n):
        @pl.loop(jnp.where(n == 0, 1, 0), pieces)
        def _(d):
            fetch(n, d).wait()
            step(n, d, x_ref[n, pl.ds(pl.multiple_of(d * CHUNK, CHUNK), CHUNK)])

    if mode == 1:
        token_ref = refs[4]
        token_ref[...] = jnp.zeros_like(token_ref)
        edge = refs[0].shape[0]
        for shift, ref in enumerate(refs[:4]):
            start = pl.multiple_of(lax.rem(meta[J_AT] + shift, 4) * edge, edge)
            ref[...] = total[pl.ds(start, edge), :].astype(ref.dtype)
    else:
        piece = refs[0].shape[2]
        for ref, core in ((refs[0], meta[CORE_AT]), (refs[1], 1 - meta[CORE_AT])):
            for k in range(NK):
                for xh in range(NX * NH):
                    start = ((xh * NC + core) * NK + k) * piece
                    ref[k, xh] = total[pl.ds(pl.multiple_of(start, piece), piece), :].astype(ref.dtype)


def mode_update(mode, meta, blocks, head, a_slab, own, other, after):
    slots, size = blocks.shape[0], blocks.shape[-1]
    slab, rank = own.shape
    vmem = pl.BlockSpec(memory_space=pltpu.VMEM)
    anywhere = pl.BlockSpec(memory_space=pl.ANY)
    if mode == 1:
        rows = (slab // NJ, rank)
        outs = [jax.ShapeDtypeStruct(rows, F32)] + [jax.ShapeDtypeStruct(rows, BF16)] * 3 + [TOKEN]
    else:
        rows = (NK, NX * NH, slab // (NK * NX * NH * NC), rank)
        outs = [jax.ShapeDtypeStruct(rows, F32), jax.ShapeDtypeStruct(rows, BF16)]
    return pl.pallas_call(
        functools.partial(mode_body, mode),
        in_specs=[pl.BlockSpec(memory_space=pltpu.SMEM), anywhere] + [vmem] * 4 + [anywhere],
        out_specs=[vmem] * len(outs),
        out_shape=outs,
        scratch_shapes=[
            pltpu.VMEM(blocks.shape, BF16),
            pltpu.VMEM((slab, rank), F32),
            pltpu.SemaphoreType.DMA((slots, size // CHUNK)),
        ],
        compiler_params=pltpu.CompilerParams(vmem_limit_bytes=48 * 2**20),
        cost_estimate=pl.CostEstimate(
            flops=MODE_FLOPS, bytes_accessed=2 * blocks.size, transcendentals=0
        ),
        name=f"mode_{mode}",
    )(meta, blocks, head, a_slab, own, other, after)


def local(blocks, coords, counts, b_factor, c_factor):
    blocks = blocks[0, 0, 0]
    ia, j, k = (lax.axis_index(name) for name in AXES)
    x, half, core = ia // (NH * NC), ia // NC % NH, ia % NC
    first = core == 0
    piece, rank = b_factor.shape[1:]
    slab = piece * NX * NH * NC * NK
    rows_a = slab * NX * NH * NC
    rows_b = slab * NJ
    rows_c = slab * NK

    mine = jnp.where(first, b_factor[0], c_factor[0])
    other = jnp.where(first, send(b_factor[0], flip_core), send(c_factor[0], flip_core))
    pair = jnp.stack([jnp.where(first, mine, other), jnp.where(first, other, mine)])
    got = send(pair, flip_half)
    quad = jnp.stack([jnp.where(half == 0, pair, got), jnp.where(half == 0, got, pair)])
    ring = ring_gather(quad, k_or_j, jnp.where(first, k, j), axis=2)
    own_slab = ring_gather(ring, along_x, x).reshape(slab, rank)
    meta = jnp.concatenate([counts.reshape(-1), coords.reshape(-1), j[None], core[None]])
    meta, head = lax.optimization_barrier((meta, blocks[0, :CHUNK]))
    ready = jnp.minimum(jnp.min(meta), 0).astype(F32) + zero_of(head[0, 0, :1].astype(F32))
    own_half = (own_slab + ready).astype(BF16)
    other_half = send(own_half, flip_core)

    gram_part = gram_of(own_slab)
    kept, *gone, token = mode_update(
        1, meta, blocks, head, own_half, own_half, other_half, gram_part
    )
    own_gram = ring_sum(gram_part, j_or_k) + token
    own_gram = own_gram * jnp.where(first, 1.0 / rows_b, 1.0 / rows_c)
    other_gram = send(own_gram, flip_core)
    gram_c = jnp.where(first, other_gram, own_gram)

    half_way, _, token = eliminate("product", (own_gram, other_gram), 0, 4)
    got = [send(g, functools.partial(along_j, i + 1)).astype(F32) for i, g in enumerate(gone)]
    m_a = (kept + got[0]) + (got[1] + got[2]) + token
    inverse_one, _, token = eliminate("plain", (half_way,), 4, 8, (m_a,))
    m_a = ring_sum(m_a, along_k, BF16) + token
    unscaled_a = dot_full(m_a, inverse_one)

    a_slab, near, far = assemble(ring_shifts(unscaled_a.astype(BF16), along_j), meta)
    part = near + send(far, flip_core)
    keep, give = mode_update(2, meta, blocks, head, a_slab, own_half, other_half, part)
    part = ring_sum(part, along_x)
    m_b = keep + send(give, flip_core).astype(F32) + zero_of(part)
    part = part + send(part, flip_half)
    m_b = ring_scatter(m_b, along_k, k, BF16)
    other = send(part, flip_core)
    inverse_two, scale_a, scale_rows = eliminate("halves", (meta, part, other, gram_c), 0, 8, (m_b,), rows_a)
    own_rows = slab // (NJ * NK)
    a_new = lax.dynamic_slice_in_dim(unscaled_a, k * own_rows, own_rows, 0) / scale_a
    m_b = jnp.sum(to_all(m_b.astype(BF16), COLUMN_GROUPS).astype(F32), axis=0)
    unscaled_b = dot_full(m_b.reshape(NX * NH * piece, rank), inverse_two) * scale_rows
    squares_b = jnp.sum(unscaled_b * unscaled_b, axis=0, keepdims=True)
    squares_b = squares_b + send(squares_b, flip_core)
    squares_b = jnp.sum(to_all(squares_b, PLANE_GROUPS), axis=0)
    b_new = lax.dynamic_slice_in_dim(unscaled_b, (x * NH + half) * piece, piece, 0)
    b_new = b_new / jnp.sqrt(squares_b / rows_b + 1e-06)
    return (a_new[None], b_new[None])


def solution(mesh):
    return jax.shard_map(
        local,
        mesh=mesh,
        in_specs=(
            P("ia", "ja", "ka", None, None, None, None),
            P("ia", "ja", "ka", None, None),
            P("ia", "ja", "ka"),
            P("ja", ("ia", "ka"), None),
            P("ka", ("ia", "ja"), None),
        ),
        out_specs=(P("ia", ("ja", "ka"), None), P("ja", ("ia", "ka"), None)),
        check_vma=False,
    )
```
